32 devices in a mesh: grid: 8 (over z, y), chan: 4 (over x, core).
Axes of the slice: x: 2, y: 2, z: 4, core: 2. Of those that a mesh axis runs over, the one named last changes fastest.
Arguments:
- spectra: bfloat16 [2, 8, 24, 4096], P(None, None, 'grid', 'chan'), may hold values from -90 to 90, as said below
- travel: int32 [32768, 4096], P('grid', 'chan'), may hold values from 0 to 2047
- quality: int32 [4096], P('chan'), may hold values 0 or 1
Outputs:
- beam_power: float32 [24, 32768], P(None, ('grid', 'chan'))
The draws below stay inside these ranges and needn't reach their ends.
Inputs may be any that keep to these rules, and one draw needn't show every extreme that they name: `spectra`: spectra of the windows; scales differ between channels and between windows.
All inputs are finite; a program needn't handle non-finite values. No bound on the sum of `quality` on one device may be relied on, other than what follows from the above.
Results may differ from the reference program's by a relative error of at most 0.0012.
Values may be sent and summed in bfloat16 or wider, within the bound.
A program may use at most 128 MiB of HBM per device.

```python
import math
import jax
import jax.numpy as jnp
from jax import lax

C = 4096
F = 8
NFFT = 2048
W = 24
G = 32768
N_CHAN = 4


def draw_spectra(key, part):
    subkeys = jax.random.split(key, 3)
    positions = jnp.arange(C, dtype=jnp.float32) / C
    rising = jnp.exp(positions * math.log(3.0))
    roughness = jnp.exp(jax.random.uniform(subkeys[1], (C,), jnp.float32, 0.0, math.log(10.0)))
    window_scale = jnp.exp(jax.random.uniform(subkeys[2], (W,), jnp.float32, math.log(0.3), math.log(3.0)))
    scales = 0.3 * window_scale[:, None] * (rising * roughness)[None, :]
    noise_part = jnp.clip(jax.random.normal(subkeys[0], (2, F, W, C), jnp.float32), -3.0, 3.0)
    drawn_values = noise_part * scales
    return drawn_values.astype(jnp.bfloat16)


def touch_ends(values, stream_key, smallest, largest):
    extent = values.shape
    spot = [jax.random.randint(jax.random.fold_in(stream_key, axis), (), 0, extent[axis]) for axis in range(len(extent))]
    values = values.at[tuple(spot)].set(smallest)
    longest = extent.index(max(extent))
    spot[longest] = (spot[longest] + 1) % extent[longest]
    return values.at[tuple(spot)].set(largest)


def setup_inputs(seed: int = 0) -> dict:
    key_of = jax.random.split(jax.random.key(seed), 4)
    return {
        "spectra": draw_spectra(jax.random.fold_in(key_of[3], 71), 0),
        "travel": touch_ends(jax.random.randint(key_of[1], (G, C), 0, 2048), jax.random.fold_in(key_of[1], 1), 0, 2047).astype(jnp.int32),
        "quality": touch_ends((jax.random.randint(key_of[2], (C,), 0, 8) < 7).astype(jnp.int32), jax.random.fold_in(key_of[2], 1), 0, 1),
    }


lowest_bin = 37
bin_spacing = 29


def replica_rows(delay_rows):
    freq_bins = lowest_bin + bin_spacing * jnp.arange(F, dtype=jnp.int32)
    phase_index = (freq_bins[:, None, None] * delay_rows[None, :, :]) % NFFT
    angles = phase_index.astype(jnp.float32) * (2.0 * math.pi / NFFT)
    return jnp.concatenate([jnp.cos(angles), jnp.sin(angles)], axis=2).astype(jnp.bfloat16)


def stacked_spectra(masked):
    real_part = masked[0]
    imag_part = masked[1]
    upper_half = jnp.concatenate([real_part, imag_part], axis=1)
    lower_half = jnp.concatenate([-imag_part, real_part], axis=1)
    return jnp.concatenate([upper_half, lower_half], axis=2)


def reference(spectra, travel, quality):
    masked = spectra * quality.astype(jnp.bfloat16)
    squared = masked.astype(jnp.float32) ** 2
    window_norm = jnp.sum(squared, axis=(0, 1, 3)) / (F * C) + 1e-6
    chan_width = C // N_CHAN
    row_count = math.gcd(G, 4096)

    def per_block(running, block_index):
        first_col = block_index * chan_width
        delay_table = lax.dynamic_slice_in_dim(travel, first_col, chan_width, 1)
        spectra_part = lax.dynamic_slice_in_dim(masked, first_col, chan_width, 3)
        spectra_matrix = stacked_spectra(spectra_part).astype(jnp.float32)

        def one_block(delay_rows):
            replicas = replica_rows(delay_rows).astype(jnp.float32)
            beam_terms = jnp.einsum("frk,fwk->rfw", replicas, spectra_matrix)
            return beam_terms.reshape(delay_rows.shape[0], -1)

        block_terms = lax.map(one_block, delay_table.reshape(G // row_count, row_count, chan_width))
        partial_beams = block_terms.reshape(G, -1)
        return running + partial_beams, None

    start_sum = jnp.zeros((G, 2 * F * W), jnp.float32)
    beams, unused = lax.scan(per_block, start_sum, jnp.arange(N_CHAN, dtype=jnp.int32))
    energies = jnp.sum(beams.reshape(G, 2 * F, W) ** 2, axis=1)
    beam_power = energies / (F * C * window_norm[None, :])
    return beam_power.T
```

```python
import functools
import math

import jax
import jax.numpy as jnp
import numpy as np
from jax import lax
from jax.experimental import pallas as pl
from jax.experimental.pallas import tpu as pltpu
from jax.sharding import PartitionSpec as P

NFFT = 2048
LANES = 128
lowest_bin = 37
bin_spacing = 29

MESH = pl.DeviceIdType.MESH


def trig_tables(freq_count):
    top_bin = lowest_bin + bin_spacing * (freq_count - 1)
    lane = np.arange(LANES, dtype=np.int64)
    rows = []
    for bin_index, stride in ((top_bin, 1), (bin_spacing, 1), (bin_spacing, LANES), (top_bin, LANES)):
        angle = 2.0 * np.pi * ((bin_index * lane * stride) % NFFT) / NFFT
        rows += [np.cos(angle), np.sin(angle)]
    return np.stack(rows).astype(np.float32)


def selection_matrix(freq_count, window_count, grid_count):
    own = window_count // grid_count
    rows = np.zeros((2, freq_count, 2, window_count, grid_count, freq_count, 2, own), np.float32)
    for f in range(freq_count):
        for w in range(window_count):
            i, v = w // own, w % own
            rows[0, f, 0, w, i, f, 0, v] = 1
            rows[0, f, 1, w, i, f, 1, v] = 1
            rows[1, f, 0, w, i, f, 1, v] = -1
            rows[1, f, 1, w, i, f, 0, v] = 1
    return rows.reshape(2 * freq_count * 2 * window_count, grid_count * freq_count * 2 * own)


def window_sums(freq_count, window_count):
    return np.tile(np.eye(window_count, dtype=np.float32), (1, 2 * freq_count))


class Sizes:
    def __init__(self, rows, chans, freq_count, window_count, grid_count, chan_count):
        self.rows, self.chans = rows, chans
        self.freqs, self.windows = freq_count, window_count
        self.grid, self.chan = grid_count, chan_count
        self.chips = chan_count // 2
        self.rows_out = rows // chan_count
        self.block = math.gcd(self.rows_out, 512)
        self.blocks = self.rows_out // self.block
        self.piece = min(256, chans // 2)
        self.pieces = chans // self.piece
        self.pairs = self.pieces // 2
        self.steps = chan_count * self.blocks
        self.cols = 2 * freq_count * window_count
        self.per_f = 2 * window_count
        self.half = freq_count // 2
        self.ranges = []
        for g in range(2):
            start, end = g * self.half * self.per_f, (g + 1) * self.half * self.per_f
            self.ranges.append((start // LANES * LANES, -(-end // LANES) * LANES))
        self.width = max(hi - lo for lo, hi in self.ranges)


def make_replicas(z, tables, delays_of, out_ref):
    top_bin = lowest_bin + bin_spacing * (z.freqs - 1)

    def look(row, index):
        return jnp.take_along_axis(
            jnp.broadcast_to(tables[row : row + 1, :], index.shape), index, axis=1, mode="promise_in_bounds"
        )

    for r in range(0, z.block, 16):
        for c in range(0, z.piece, LANES):
            delay = delays_of(r, c)
            low = delay & (LANES - 1)
            high = delay >> 7
            cl, sl, ch, sh = look(2, low), look(3, low), look(4, high), look(5, high)
            cb = cl * ch - sl * sh
            sb = sl * ch + cl * sh
            c1, s1 = look(0, low), look(1, low)
            if (top_bin * LANES) % NFFT:
                ct, st = look(6, high), look(7, high)
                c1, s1 = c1 * ct - s1 * st, s1 * ct + c1 * st
            c0 = c1 * cb + s1 * sb
            s0 = s1 * cb - c1 * sb
            twice = cb + cb
            for f in reversed(range(z.freqs)):
                col = 2 * f * z.piece + c
                out_ref[r : r + 16, col : col + LANES] = c1.astype(jnp.bfloat16)
                out_ref[r : r + 16, col + z.piece : col + z.piece + LANES] = s1.astype(jnp.bfloat16)
                if f:
                    c1, c0 = c0, twice * c0 - c1
                    s1, s0 = s0, twice * s0 - s1


def kernel(z, gathered, select, tables, sums, travel, out,
           weights, rep_a, rep_b, delays, acc, mate_out, mate_in, chip_out, chip_in, norms,
           delay_sem, mate_send, mate_recv, chip_send, chip_recv, norm_send, norm_recv):
    me = lax.axis_index("chan")
    chip, core = me // 2, lax.rem(me, 2)
    mate = chip * 2 + 1 - core
    half_cols = 2 * z.half * z.piece

    barrier = pltpu.get_barrier_semaphore()
    for k in range(1, z.chan):
        pl.semaphore_signal(barrier, inc=1, device_id={"chan": lax.rem(me + k, z.chan)}, device_id_type=MESH)

    def chip_at(j):
        return lax.rem(chip + 1 + j, z.chips)

    def row_start(step):
        phase, block = step // z.blocks, lax.rem(step, z.blocks)
        j, kind = phase // 2, lax.rem(phase, 2)
        quarter = chip_at(j) * 2 + jnp.where(kind == 0, 1 - core, core)
        return pl.multiple_of(quarter * z.rows_out + block * z.block, z.block)

    def delay_copy(step):
        slot = lax.rem(step, 2)
        return pltpu.make_async_copy(
            travel.at[pl.ds(row_start(step), z.block), :], delays.at[slot], delay_sem.at[slot]
        )

    delay_copy(0).start()

    weights[...] = jnp.zeros_like(weights)
    sum_sq = jnp.zeros((z.windows, LANES), jnp.float32)
    for trig in range(2):
        for f in range(z.freqs):
            g, at = f // z.half, f % z.half
            first = (trig * z.freqs + f) * z.per_f
            part = jnp.dot(
                select[first : first + z.per_f, :], gathered[...], preferred_element_type=jnp.float32
            )
            if trig == 0:
                squared = part * part
                lanes = squared[:, 0:LANES]
                for c in range(LANES, z.chans, LANES):
                    lanes += squared[:, c : c + LANES]
                sum_sq += lanes[: z.windows] + lanes[z.windows :]
            part = part.astype(jnp.bfloat16)
            row = f * z.per_f - z.ranges[g][0]
            for p in range(z.pieces):
                col = (2 * at + trig) * z.piece
                weights[g, p, row : row + z.per_f, col : col + z.piece] = part[:, p * z.piece : (p + 1) * z.piece]
    norms[0] = sum_sq

    acc[...] = jnp.zeros_like(acc)
    delay_copy(0).wait()
    pl.semaphore_wait(barrier, z.chan - 1)

    def norm_copy(k):
        return pltpu.make_async_remote_copy(
            src_ref=norms.at[0], dst_ref=norms.at[k], send_sem=norm_send.at[k], recv_sem=norm_recv.at[k],
            device_id={"chan": lax.rem(me + k, z.chan)}, device_id_type=MESH,
        )

    for k in range(1, z.chan):
        norm_copy(k).start()

    def mate_copy(j, block):
        return pltpu.make_async_remote_copy(
            src_ref=mate_out.at[j, block], dst_ref=mate_in.at[j, block],
            send_sem=mate_send.at[j, block], recv_sem=mate_recv.at[j, block],
            device_id={"chan": mate}, device_id_type=MESH,
        )

    def chip_copy(j, block):
        return pltpu.make_async_remote_copy(
            src_ref=chip_out.at[j, block], dst_ref=chip_in.at[j, block],
            send_sem=chip_send.at[j, block], recv_sem=chip_recv.at[j, block],
            device_id={"chan": chip_at(j) * 2 + core}, device_id_type=MESH,
        )

    def multiply(rep, p):
        for g in range(2):
            lo, hi = z.ranges[g]
            acc[:, lo:hi] += lax.dot_general(
                rep[:, g * half_cols : (g + 1) * half_cols], weights[g, p, 0 : hi - lo, :],
                (((1,), (1,)), ((), ())), preferred_element_type=jnp.float32,
            )

    def replicas(slot, p, rep):
        def delays_of(r, c):
            return delays[slot, r : r + 16, pl.ds(pl.multiple_of(p * z.piece + c, LANES), LANES)]

        make_replicas(z, tables, delays_of, rep)

    replicas(0, 0, rep_a)

    def pair_step(it, carry):
        step, pair = it // z.pairs, lax.rem(it, z.pairs)
        slot = lax.rem(step, 2)
        after = jnp.minimum(it + 1, z.steps * z.pairs - 1)
        step2, pair2 = after // z.pairs, lax.rem(after, z.pairs)

        @pl.when((pair == 0) & (step + 1 < z.steps))
        def _():
            delay_copy(step + 1).start()

        multiply(rep_a, 2 * pair)
        replicas(slot, 2 * pair + 1, rep_b)

        @pl.when(step2 != step)
        def _():
            delay_copy(step2).wait()

        multiply(rep_b, 2 * pair + 1)
        replicas(lax.rem(step2, 2), 2 * pair2, rep_a)

        @pl.when(pair == z.pairs - 1)
        def _():
            phase, block = step // z.blocks, lax.rem(step, z.blocks)
            j, kind = phase // 2, lax.rem(phase, 2)

            @pl.when(kind == 0)
            def _():
                mate_out[j, block] = acc[...]
                mate_copy(j, block).start()

            @pl.when((kind == 1) & (j < z.chips - 1))
            def _():
                mate_copy(j, block).wait_recv()
                chip_out[j, block] = (acc[...] + mate_in[j, block]).astype(jnp.bfloat16)
                chip_copy(j, block).start()

            @pl.when((kind == 1) & (j == z.chips - 1))
            def _():
                mate_copy(z.chips - 1, block).wait_recv()
                beams = acc[...] + mate_in[z.chips - 1, block]
                for k in range(z.chips - 1):
                    chip_copy(k, block).wait_recv()
                    beams += chip_in[k, block].astype(jnp.float32)
                power = beams * beams
                high = power.astype(jnp.bfloat16)
                low = (power - high.astype(jnp.float32)).astype(jnp.bfloat16)
                dims = (((1,), (1,)), ((), ()))
                energy = lax.dot_general(sums[...], high, dims, preferred_element_type=jnp.float32)
                energy += lax.dot_general(sums[...], low, dims, preferred_element_type=jnp.float32)
                out[:, pl.ds(pl.multiple_of(block * z.block, z.block), z.block)] = energy

            acc[...] = jnp.zeros_like(acc)

        return carry

    lax.fori_loop(0, z.steps * z.pairs, pair_step, 0)

    for k in range(1, z.chan):
        norm_copy(k).wait()
    total = norms[0]
    for k in range(1, z.chan):
        total += norms[k]
    scale = z.freqs * z.chans * z.chan
    window_norm = jnp.sum(total, axis=1, keepdims=True) / scale + 1e-06
    out[...] = out[...] / (scale * window_norm)

    for j in range(z.chips):
        for block in range(z.blocks):
            mate_copy(j, block).wait_send()
            if j < z.chips - 1:
                chip_copy(j, block).wait_send()


def per_device(spectra, travel, quality):
    _, freq_count, own, chans = spectra.shape
    grid_count, chan_count = lax.axis_size("grid"), lax.axis_size("chan")
    z = Sizes(travel.shape[0], chans, freq_count, own * grid_count, grid_count, chan_count)
    masked = spectra * quality.astype(jnp.bfloat16)
    mine = jnp.transpose(masked, (1, 0, 2, 3)).reshape(2 * freq_count * own, chans)
    gathered = lax.all_gather(mine, "grid", axis=0, tiled=True)
    select = jnp.asarray(selection_matrix(freq_count, z.windows, grid_count), jnp.bfloat16)
    tables = jnp.asarray(trig_tables(freq_count))
    sums = jnp.asarray(window_sums(freq_count, z.windows), jnp.bfloat16)
    vmem = pl.BlockSpec(memory_space=pltpu.VMEM)
    far = max(z.chips - 1, 1)
    flops = 2 * z.rows * z.chans * z.cols * 2
    return pl.pallas_call(
        functools.partial(kernel, z),
        out_shape=jax.ShapeDtypeStruct((z.windows, z.rows_out), jnp.float32),
        in_specs=[vmem, vmem, vmem, vmem, pl.BlockSpec(memory_space=pl.ANY)],
        out_specs=vmem,
        scratch_shapes=[
            pltpu.VMEM((2, z.pieces, z.width, 2 * z.half * z.piece), jnp.bfloat16),
            pltpu.VMEM((z.block, 2 * z.freqs * z.piece), jnp.bfloat16),
            pltpu.VMEM((z.block, 2 * z.freqs * z.piece), jnp.bfloat16),
            pltpu.VMEM((2, z.block, z.chans), jnp.int32),
            pltpu.VMEM((z.block, z.cols), jnp.float32),
            pltpu.VMEM((z.chips, z.blocks, z.block, z.cols), jnp.float32),
            pltpu.VMEM((z.chips, z.blocks, z.block, z.cols), jnp.float32),
            pltpu.VMEM((far, z.blocks, z.block, z.cols), jnp.bfloat16),
            pltpu.VMEM((far, z.blocks, z.block, z.cols), jnp.bfloat16),
            pltpu.VMEM((z.chan, z.windows, LANES), jnp.float32),
            pltpu.SemaphoreType.DMA((2,)),
            pltpu.SemaphoreType.DMA((z.chips, z.blocks)),
            pltpu.SemaphoreType.DMA((z.chips, z.blocks)),
            pltpu.SemaphoreType.DMA((far, z.blocks)),
            pltpu.SemaphoreType.DMA((far, z.blocks)),
            pltpu.SemaphoreType.DMA((z.chan,)),
            pltpu.SemaphoreType.DMA((z.chan,)),
        ],
        compiler_params=pltpu.CompilerParams(
            collective_id=0, has_side_effects=True, vmem_limit_bytes=56 * 1024 * 1024
        ),
        cost_estimate=pl.CostEstimate(
            flops=flops, bytes_accessed=4 * z.rows * z.chans, transcendentals=0
        ),
        name="beam_power",
    )(gathered, select, tables, sums, travel)


def solution(mesh):
    return jax.shard_map(
        per_device,
        mesh=mesh,
        in_specs=(P(None, None, "grid", "chan"), P("grid", "chan"), P("chan")),
        out_specs=P(None, ("grid", "chan")),
        check_vma=False,
    )
```

```python
import functools
import math

import jax
import jax.numpy as jnp
import numpy as np
from jax import lax
from jax.experimental import pallas as pl
from jax.experimental.pallas import tpu as pltpu
from jax.sharding import PartitionSpec as P

NFFT = 2048
LANES = 128
lowest_bin = 37
bin_spacing = 29

MESH = pl.DeviceIdType.MESH


def trig_tables(freq_count):
    top_bin = lowest_bin + bin_spacing * (freq_count - 1)
    lane = np.arange(LANES, dtype=np.int64)
    rows = []
    for bin_index, stride in ((top_bin, 1), (bin_spacing, 1), (bin_spacing, LANES), (top_bin, LANES)):
        angle = 2.0 * np.pi * ((bin_index * lane * stride) % NFFT) / NFFT
        rows += [np.cos(angle), np.sin(angle)]
    return np.stack(rows).astype(np.float32)


def selection_matrix(z):
    own = z.windows // z.grid
    cols = np.zeros((2, z.grid, 2, own, z.freqs, z.freqs, 2, z.windows), np.float32)
    for f in range(z.freqs):
        for w in range(z.windows):
            i, v = w // own, w % own
            cols[0, i, 0, v, f, f, 0, w] = 1
            cols[0, i, 1, v, f, f, 1, w] = 1
            cols[1, i, 1, v, f, f, 0, w] = -1
            cols[1, i, 0, v, f, f, 1, w] = 1
    cols = cols.reshape(2, -1, z.cols)
    halves = np.zeros((2, 2, cols.shape[1], z.width), np.float32)
    for g in range(2):
        lo, hi = z.ranges[g]
        start = g * z.half * z.per_f
        end = start + z.half * z.per_f
        halves[g, :, :, start - lo : end - lo] = cols[:, :, start:end]
    return halves


def window_sums(freq_count, window_count):
    return np.tile(np.eye(window_count, dtype=np.float32), (1, 2 * freq_count))


def split_dot(left, values, terms):
    total = None
    for _ in range(terms):
        term = values.astype(jnp.bfloat16)
        product = lax.dot_general(left, term, (((1,), (1,)), ((), ())), preferred_element_type=jnp.float32)
        total = product if total is None else total + product
        values = values - term.astype(jnp.float32)
    return total


class Sizes:
    def __init__(self, rows, chans, freq_count, window_count, grid_count, chan_count):
        self.rows, self.chans = rows, chans
        self.freqs, self.windows = freq_count, window_count
        self.grid, self.chan = grid_count, chan_count
        self.chips = chan_count // 2
        self.rows_out = rows // chan_count
        self.block = math.gcd(self.rows_out, 512)
        self.blocks = self.rows_out // self.block
        self.piece = min(256, chans // 2)
        self.pieces = chans // self.piece
        self.pairs = self.pieces // 2
        self.steps = chan_count * self.blocks
        self.total = self.steps * self.pieces
        self.lead = min(5, self.total - 1)
        self.slots = (self.lead + 1) // 2
        self.cols = 2 * freq_count * window_count
        self.per_f = 2 * window_count
        self.half = freq_count // 2
        self.ranges = []
        for g in range(2):
            start, end = g * self.half * self.per_f, (g + 1) * self.half * self.per_f
            self.ranges.append((start // LANES * LANES, -(-end // LANES) * LANES))
        self.width = max(hi - lo for lo, hi in self.ranges)


def make_replicas(z, tables, delays_of, out_ref, slot, rows):
    top_bin = lowest_bin + bin_spacing * (z.freqs - 1)

    def look(row, index):
        return jnp.take_along_axis(
            jnp.broadcast_to(tables[row : row + 1, :], index.shape), index, axis=1, mode="promise_in_bounds"
        )

    for r in range(rows[0], rows[1], 16):
        for c in range(0, z.piece, LANES):
            delay = delays_of(r, c)
            low = delay & (LANES - 1)
            high = delay >> 7
            cl, sl, c1, s1 = look(2, low), look(3, low), look(0, low), look(1, low)
            ch, sh = look(4, high), look(5, high)
            cb = cl * ch - sl * sh
            sb = sl * ch + cl * sh
            if (top_bin * LANES) % NFFT:
                ct, st = look(6, high), look(7, high)
                c1, s1 = c1 * ct - s1 * st, s1 * ct + c1 * st
            c0 = c1 * cb + s1 * sb
            s0 = s1 * cb - c1 * sb
            twice = cb + cb
            for f in reversed(range(z.freqs)):
                col = 2 * f * z.piece + c
                out_ref[slot, r : r + 16, col : col + LANES] = c1.astype(jnp.bfloat16)
                out_ref[slot, r : r + 16, col + z.piece : col + z.piece + LANES] = s1.astype(jnp.bfloat16)
                if f:
                    c1, c0 = c0, twice * c0 - c1
                    s1, s0 = s0, twice * s0 - s1


def kernel(z, spectra, quality, select, tables, sums, travel, out,
           gathered, weights, rep_even, rep_odd, delays, acc, mate_out, mate_in, chip_out, chip_in, norms,
           own_send, own_recv, pass_send, pass_recv,
           delay_sem, mate_send, mate_recv, chip_send, chip_recv, norm_send, norm_recv):
    me = lax.axis_index("chan")
    slab = lax.axis_index("grid")
    chip, core = me // 2, lax.rem(me, 2)
    mate = chip * 2 + 1 - core
    next_slab = slab + 1 - 2 * lax.rem(slab, 2)
    far_slabs = z.grid // 2
    half_cols = 2 * z.half * z.piece

    barrier = pltpu.get_barrier_semaphore()
    for k in range(1, z.chan):
        pl.semaphore_signal(barrier, inc=1, device_id={"chan": lax.rem(me + k, z.chan)}, device_id_type=MESH)
    for k in range(1, far_slabs):
        pl.semaphore_signal(barrier, inc=1, device_id={"grid": lax.rem(slab + 2 * k, z.grid)}, device_id_type=MESH)
    pl.semaphore_signal(barrier, inc=1, device_id={"grid": next_slab}, device_id_type=MESH)

    def chip_at(j):
        return lax.rem(chip + 1 + j, z.chips)

    def row_start(step):
        phase, block = step // z.blocks, lax.rem(step, z.blocks)
        j, kind = phase // 2, lax.rem(phase, 2)
        quarter = chip_at(j) * 2 + jnp.where(kind == 0, 1 - core, core)
        return pl.multiple_of(quarter * z.rows_out + block * z.block, z.block)

    def delay_copy(step):
        slot = lax.rem(step, 2)
        return pltpu.make_async_copy(
            travel.at[pl.ds(row_start(step), z.block), :], delays.at[slot], delay_sem.at[slot]
        )

    delay_copy(0).start()
    delay_copy(1).start()

    gathered[slab] = spectra[...] * quality[...].astype(jnp.bfloat16)
    pl.semaphore_wait(barrier, z.chan - 1 + far_slabs)

    def own_copy(k):
        target = next_slab if k == 0 else lax.rem(slab + 2 * k, z.grid)
        return pltpu.make_async_remote_copy(
            src_ref=gathered.at[slab], dst_ref=gathered.at[slab],
            send_sem=own_send.at[k], recv_sem=own_recv.at[k],
            device_id={"grid": target}, device_id_type=MESH,
        )

    def own_arrival(k):
        source = next_slab if isinstance(k, int) and k == 0 else lax.rem(slab + z.grid - 2 * k, z.grid)
        return pltpu.make_async_remote_copy(
            src_ref=gathered.at[source], dst_ref=gathered.at[source],
            send_sem=own_send.at[k], recv_sem=own_recv.at[k],
            device_id={"grid": next_slab}, device_id_type=MESH,
        )

    def pass_copy(k):
        source = lax.rem(slab + z.grid - 2 * k, z.grid)
        return pltpu.make_async_remote_copy(
            src_ref=gathered.at[source], dst_ref=gathered.at[source],
            send_sem=pass_send.at[k], recv_sem=pass_recv.at[k],
            device_id={"grid": next_slab}, device_id_type=MESH,
        )

    def pass_arrival(k):
        source = lax.rem(next_slab + z.grid - 2 * k, z.grid)
        return pltpu.make_async_remote_copy(
            src_ref=gathered.at[source], dst_ref=gathered.at[source],
            send_sem=pass_send.at[k], recv_sem=pass_recv.at[k],
            device_id={"grid": next_slab}, device_id_type=MESH,
        )

    near_first = sorted(range(1, far_slabs), key=lambda k: min(k, far_slabs - k))
    for k in near_first:
        own_copy(k).start()
    own_copy(0).start()

    def replicas(piece, rep, rows):
        slot, p = lax.rem(piece // z.pieces, 2), lax.rem(piece, z.pieces)

        def delays_of(r, c):
            return delays[slot, r : r + 16, pl.ds(pl.multiple_of(p * z.piece + c, LANES), LANES)]

        make_replicas(z, tables, delays_of, rep, lax.rem(piece // 2, z.slots), rows)

    def delays_ready(piece):
        @pl.when(lax.rem(piece, z.pieces) == 0)
        def _():
            delay_copy(piece // z.pieces).wait()

    def delays_used(piece):
        after = piece // z.pieces + 2

        @pl.when((lax.rem(piece, z.pieces) == z.pieces - 1) & (after < z.steps))
        def _():
            delay_copy(after).start()

    def early(piece, carry):
        @pl.when(lax.rem(piece, 2) == 0)
        def _():
            delays_ready(piece)
            replicas(piece, rep_even, (0, z.block))

        @pl.when(lax.rem(piece, 2) == 1)
        def _():
            replicas(piece, rep_odd, (0, z.block))
            delays_used(piece)

        return carry

    spots = [z.lead * (n + 1) // (len(near_first) + 2) for n in range(len(near_first))]
    done = 0
    for k, spot in zip(near_first, spots):
        if spot > done:
            lax.fori_loop(done, spot, early, 0)
            done = spot
        own_arrival(k).wait_recv()
        pass_copy(k).start()
    lax.fori_loop(done, z.lead, early, 0)

    own_arrival(0).wait_recv()
    for k in near_first:
        pass_arrival(k).wait_recv()

    spectra_rows = gathered[...].reshape(z.grid * gathered.shape[1], z.chans)
    for g in range(2):
        lo, hi = z.ranges[g]
        lane = lax.broadcasted_iota(jnp.int32, (z.piece, hi - lo), 1) + lo
        sum_sq = jnp.zeros((8, hi - lo), jnp.float32)
        for trig in range(2):
            for p in range(z.pieces):
                part = lax.dot_general(
                    spectra_rows[:, p * z.piece : (p + 1) * z.piece], select[g, trig, :, 0 : hi - lo],
                    (((0,), (0,)), ((), ())), preferred_element_type=jnp.float32,
                )
                if trig == 0:
                    sum_sq += jnp.sum((part * part).reshape(z.piece // 8, 8, hi - lo), axis=0)
                for at in range(z.half):
                    first = (g * z.half + at) * z.per_f
                    row = (2 * at + trig) * z.piece
                    chosen = jnp.where((lane >= first) & (lane < first + z.per_f), part, 0.0)
                    weights[g, p, row : row + z.piece, 0 : hi - lo] = chosen.astype(jnp.bfloat16)
        if g == 0:
            norms[0, :, lo:hi] = sum_sq
            norms[0, :, hi:] = jnp.zeros((8, z.cols - hi), jnp.float32)
        else:
            norms[0, :, lo:hi] += sum_sq

    acc[...] = jnp.zeros_like(acc)

    def norm_copy(k):
        return pltpu.make_async_remote_copy(
            src_ref=norms.at[0], dst_ref=norms.at[k], send_sem=norm_send.at[k], recv_sem=norm_recv.at[k],
            device_id={"chan": lax.rem(me + k, z.chan)}, device_id_type=MESH,
        )

    for k in range(1, z.chan):
        norm_copy(k).start()

    def mate_copy(j, block):
        return pltpu.make_async_remote_copy(
            src_ref=mate_out.at[j, block], dst_ref=mate_in.at[j, block],
            send_sem=mate_send.at[j, block], recv_sem=mate_recv.at[j, block],
            device_id={"chan": mate}, device_id_type=MESH,
        )

    def chip_copy(j, block):
        return pltpu.make_async_remote_copy(
            src_ref=chip_out.at[j, block], dst_ref=chip_in.at[j, block],
            send_sem=chip_send.at[j, block], recv_sem=chip_recv.at[j, block],
            device_id={"chan": chip_at(j) * 2 + core}, device_id_type=MESH,
        )

    def multiply(rep, piece, during):
        slot, p = lax.rem(piece // 2, z.slots), lax.rem(piece, z.pieces)
        for g in range(2):
            lo, hi = z.ranges[g]
            acc[:, lo:hi] += lax.dot_general(
                rep[slot, :, g * half_cols : (g + 1) * half_cols], weights[g, p, :, 0 : hi - lo],
                (((1,), (0,)), ((), ())), preferred_element_type=jnp.float32,
            )
            during(g)

    def turn(piece, rep, ahead_rep):
        ahead = piece + z.lead

        @pl.when(ahead < z.total)
        def _():
            def during(g):
                replicas(ahead, ahead_rep, (g * z.block // 2, (g + 1) * z.block // 2))

            multiply(rep, piece, during)

        @pl.when(ahead >= z.total)
        def _():
            multiply(rep, piece, lambda g: None)

    def pair_step(it, carry):
        step, pair = it // z.pairs, lax.rem(it, z.pairs)

        turn(2 * it, rep_even, rep_odd)
        delays_used(2 * it + z.lead)

        @pl.when(2 * it + 1 + z.lead < z.total)
        def _():
            delays_ready(2 * it + 1 + z.lead)

        turn(2 * it + 1, rep_odd, rep_even)

        @pl.when(pair == z.pairs - 1)
        def _():
            phase, block = step // z.blocks, lax.rem(step, z.blocks)
            j, kind = phase // 2, lax.rem(phase, 2)

            @pl.when(kind == 0)
            def _():
                mate_out[j, block] = acc[...]
                mate_copy(j, block).start()

            @pl.when((kind == 1) & (j < z.chips - 1))
            def _():
                mate_copy(j, block).wait_recv()
                chip_out[j, block] = (acc[...] + mate_in[j, block]).astype(jnp.bfloat16)
                chip_copy(j, block).start()

            @pl.when((kind == 1) & (j == z.chips - 1))
            def _():
                mate_copy(z.chips - 1, block).wait_recv()
                beams = acc[...] + mate_in[z.chips - 1, block]
                for k in range(z.chips - 1):
                    chip_copy(k, block).wait_recv()
                    beams += chip_in[k, block].astype(jnp.float32)
                energy = split_dot(sums[...], beams * beams, 2)
                out[:, pl.ds(pl.multiple_of(block * z.block, z.block), z.block)] = energy

            acc[...] = jnp.zeros_like(acc)

        return carry

    lax.fori_loop(0, z.steps * z.pairs, pair_step, 0)

    for k in range(1, z.chan):
        norm_copy(k).wait()
    total = norms[0]
    for k in range(1, z.chan):
        total += norms[k]
    scale = z.freqs * z.chans * z.chan
    window_norm = jnp.sum(split_dot(sums[...], total, 3), axis=1, keepdims=True) / scale + 1e-06
    out[...] = out[...] / (scale * window_norm)

    own_copy(0).wait_send()
    for k in near_first:
        own_copy(k).wait_send()
        pass_copy(k).wait_send()
    for j in range(z.chips):
        for block in range(z.blocks):
            mate_copy(j, block).wait_send()
            if j < z.chips - 1:
                chip_copy(j, block).wait_send()


def per_device(spectra, travel, quality):
    _, freq_count, own, chans = spectra.shape
    grid_count, chan_count = lax.axis_size("grid"), lax.axis_size("chan")
    z = Sizes(travel.shape[0], chans, freq_count, own * grid_count, grid_count, chan_count)
    mine = jnp.transpose(spectra, (0, 2, 1, 3)).reshape(2 * own * freq_count, chans)
    select = jnp.asarray(selection_matrix(z), jnp.bfloat16)
    tables = jnp.asarray(trig_tables(freq_count))
    sums = jnp.asarray(window_sums(freq_count, z.windows), jnp.bfloat16)
    vmem = pl.BlockSpec(memory_space=pltpu.VMEM)
    far = max(z.chips - 1, 1)
    flops = 2 * z.rows * z.chans * z.cols * 2
    return pl.pallas_call(
        functools.partial(kernel, z),
        out_shape=jax.ShapeDtypeStruct((z.windows, z.rows_out), jnp.float32),
        in_specs=[vmem, vmem, vmem, vmem, vmem, pl.BlockSpec(memory_space=pl.ANY)],
        out_specs=vmem,
        scratch_shapes=[
            pltpu.VMEM((grid_count, 2 * own * freq_count, chans), jnp.bfloat16),
            pltpu.VMEM((2, z.pieces, 2 * z.half * z.piece, z.width), jnp.bfloat16),
            pltpu.VMEM((z.slots, z.block, 2 * z.freqs * z.piece), jnp.bfloat16),
            pltpu.VMEM((z.slots, z.block, 2 * z.freqs * z.piece), jnp.bfloat16),
            pltpu.VMEM((2, z.block, z.chans), jnp.int32),
            pltpu.VMEM((z.block, z.cols), jnp.float32),
            pltpu.VMEM((z.chips, z.blocks, z.block, z.cols), jnp.float32),
            pltpu.VMEM((z.chips, z.blocks, z.block, z.cols), jnp.float32),
            pltpu.VMEM((far, z.blocks, z.block, z.cols), jnp.bfloat16),
            pltpu.VMEM((far, z.blocks, z.block, z.cols), jnp.bfloat16),
            pltpu.VMEM((z.chan, 8, z.cols), jnp.float32),
            pltpu.SemaphoreType.DMA((grid_count // 2,)),
            pltpu.SemaphoreType.DMA((grid_count // 2,)),
            pltpu.SemaphoreType.DMA((grid_count // 2,)),
            pltpu.SemaphoreType.DMA((grid_count // 2,)),
            pltpu.SemaphoreType.DMA((2,)),
            pltpu.SemaphoreType.DMA((z.chips, z.blocks)),
            pltpu.SemaphoreType.DMA((z.chips, z.blocks)),
            pltpu.SemaphoreType.DMA((far, z.blocks)),
            pltpu.SemaphoreType.DMA((far, z.blocks)),
            pltpu.SemaphoreType.DMA((z.chan,)),
            pltpu.SemaphoreType.DMA((z.chan,)),
        ],
        compiler_params=pltpu.CompilerParams(
            collective_id=0, has_side_effects=True, vmem_limit_bytes=56 * 1024 * 1024
        ),
        cost_estimate=pl.CostEstimate(
            flops=flops, bytes_accessed=4 * z.rows * z.chans, transcendentals=0
        ),
        name="beam_power",
    )(mine, quality.reshape(1, chans), select, tables, sums, travel)


def solution(mesh):
    return jax.shard_map(
        per_device,
        mesh=mesh,
        in_specs=(P(None, None, "grid", "chan"), P("grid", "chan"), P("chan")),
        out_specs=P(None, ("grid", "chan")),
        check_vma=False,
    )
```

```python
import functools
import math

import jax
import jax.numpy as jnp
import numpy as np
from jax import lax
from jax.experimental import pallas as pl
from jax.experimental.pallas import tpu as pltpu
from jax.sharding import PartitionSpec as P

NFFT = 2048
LANES = 128
lowest_bin = 37
bin_spacing = 29

MESH = pl.DeviceIdType.MESH


SINE = (6.28318527371, -10.335419365544, 5.100139396896, -1.1964839648, 0.155120274432)
COSINE = (0.999999953467, -4.934792858676, 4.05841189832, -1.331880161216, 0.219696798464)


def polynomial(square, coefficients):
    value = coefficients[-1]
    for coefficient in coefficients[-2::-1]:
        value = value * square + coefficient
    return value


def trig_tables(freq_count):
    top_bin = lowest_bin + bin_spacing * (freq_count - 1)
    lane = np.arange(LANES, dtype=np.int64)
    rows = []
    for stride in (1, LANES):
        angle = 2.0 * np.pi * ((top_bin * lane * stride) % NFFT) / NFFT
        rows += [np.cos(angle), np.sin(angle)]
    return np.stack(rows).astype(np.float32)


def selection_matrix(z):
    own = z.windows // z.grid
    cols = np.zeros((2, z.grid, 2, own, z.freqs, z.freqs, 2, z.windows), np.float32)
    for f in range(z.freqs):
        for w in range(z.windows):
            i, v = w // own, w % own
            cols[0, i, 0, v, f, f, 0, w] = 1
            cols[0, i, 1, v, f, f, 1, w] = 1
            cols[1, i, 1, v, f, f, 0, w] = -1
            cols[1, i, 0, v, f, f, 1, w] = 1
    cols = cols.reshape(2, -1, z.cols)
    halves = np.zeros((2, 2, cols.shape[1], z.width), np.float32)
    for g in range(2):
        lo, hi = z.ranges[g]
        start = g * z.half * z.per_f
        end = start + z.half * z.per_f
        halves[g, :, :, start - lo : end - lo] = cols[:, :, start:end]
    return halves


def window_sums(freq_count, window_count):
    return np.tile(np.eye(window_count, dtype=np.float32), (1, 2 * freq_count))


def split_dot(left, values, terms):
    total = None
    for _ in range(terms):
        term = values.astype(jnp.bfloat16)
        product = lax.dot_general(left, term, (((1,), (1,)), ((), ())), preferred_element_type=jnp.float32)
        total = product if total is None else total + product
        values = values - term.astype(jnp.float32)
    return total


class Sizes:
    def __init__(self, rows, chans, freq_count, window_count, grid_count, chan_count):
        self.rows, self.chans = rows, chans
        self.freqs, self.windows = freq_count, window_count
        self.grid, self.chan = grid_count, chan_count
        self.chips = chan_count // 2
        self.rows_out = rows // chan_count
        self.block = math.gcd(self.rows_out, 512)
        self.blocks = self.rows_out // self.block
        self.piece = min(256, chans // 2)
        self.pieces = chans // self.piece
        self.pairs = self.pieces // 2
        self.steps = chan_count * self.blocks
        self.total = self.steps * self.pieces
        self.lead = min(5, self.total - 1)
        self.slots = (self.lead + 1) // 2
        self.cols = 2 * freq_count * window_count
        self.per_f = 2 * window_count
        self.half = freq_count // 2
        self.ranges = []
        for g in range(2):
            start, end = g * self.half * self.per_f, (g + 1) * self.half * self.per_f
            self.ranges.append((start // LANES * LANES, -(-end // LANES) * LANES))
        self.width = max(hi - lo for lo, hi in self.ranges)


def make_replicas(z, tables, delays_of, out_ref, slot, rows):
    top_bin = lowest_bin + bin_spacing * (z.freqs - 1)

    def look(row, index):
        return jnp.take_along_axis(
            jnp.broadcast_to(tables[row : row + 1, :], index.shape), index, axis=1, mode="promise_in_bounds"
        )

    for r in range(rows[0], rows[1], 16):
        for c in range(0, z.piece, LANES):
            delay = delays_of(r, c)
            low = delay & (LANES - 1)
            c1, s1 = look(0, low), look(1, low)
            if (top_bin * LANES) % NFFT:
                high = delay >> 7
                ct, st = look(2, high), look(3, high)
                c1, s1 = c1 * ct - s1 * st, s1 * ct + c1 * st
            turns = delay.astype(jnp.float32) * (bin_spacing / NFFT)
            u = turns - lax.round(turns, lax.RoundingMethod.TO_NEAREST_EVEN)
            square = u * u
            twice_sin = u * polynomial(square, SINE)
            twice = 2.0 - twice_sin * twice_sin
            cb = 0.5 * twice
            sb = twice_sin * polynomial(square, COSINE)
            c0 = c1 * cb + s1 * sb
            s0 = s1 * cb - c1 * sb
            for f in reversed(range(z.freqs)):
                col = 2 * f * z.piece + c
                out_ref[slot, r : r + 16, col : col + LANES] = c1.astype(jnp.bfloat16)
                out_ref[slot, r : r + 16, col + z.piece : col + z.piece + LANES] = s1.astype(jnp.bfloat16)
                if f:
                    c1, c0 = c0, twice * c0 - c1
                    s1, s0 = s0, twice * s0 - s1


def kernel(z, spectra, quality, select, tables, sums, travel, out,
           gathered, weights, rep_even, rep_odd, delays, acc, mate_out, mate_in, chip_out, chip_in, norms,
           own_send, own_recv, pass_send, pass_recv,
           delay_sem, mate_send, mate_recv, chip_send, chip_recv, norm_send, norm_recv):
    me = lax.axis_index("chan")
    slab = lax.axis_index("grid")
    chip, core = me // 2, lax.rem(me, 2)
    mate = chip * 2 + 1 - core
    next_slab = slab + 1 - 2 * lax.rem(slab, 2)
    far_slabs = z.grid // 2
    half_cols = 2 * z.half * z.piece

    barrier = pltpu.get_barrier_semaphore()
    for k in range(1, z.chan):
        pl.semaphore_signal(barrier, inc=1, device_id={"chan": lax.rem(me + k, z.chan)}, device_id_type=MESH)
    for k in range(1, far_slabs):
        pl.semaphore_signal(barrier, inc=1, device_id={"grid": lax.rem(slab + 2 * k, z.grid)}, device_id_type=MESH)
    pl.semaphore_signal(barrier, inc=1, device_id={"grid": next_slab}, device_id_type=MESH)

    def chip_at(j):
        return lax.rem(chip + 1 + j, z.chips)

    def row_start(step):
        phase, block = step // z.blocks, lax.rem(step, z.blocks)
        j, kind = phase // 2, lax.rem(phase, 2)
        quarter = chip_at(j) * 2 + jnp.where(kind == 0, 1 - core, core)
        return pl.multiple_of(quarter * z.rows_out + block * z.block, z.block)

    def delay_copy(step):
        slot = lax.rem(step, 2)
        return pltpu.make_async_copy(
            travel.at[pl.ds(row_start(step), z.block), :], delays.at[slot], delay_sem.at[slot]
        )

    delay_copy(0).start()
    delay_copy(1).start()

    gathered[slab] = spectra[...] * quality[...].astype(jnp.bfloat16)
    pl.semaphore_wait(barrier, z.chan - 1 + far_slabs)

    def own_copy(k):
        target = next_slab if k == 0 else lax.rem(slab + 2 * k, z.grid)
        return pltpu.make_async_remote_copy(
            src_ref=gathered.at[slab], dst_ref=gathered.at[slab],
            send_sem=own_send.at[k], recv_sem=own_recv.at[k],
            device_id={"grid": target}, device_id_type=MESH,
        )

    def own_arrival(k):
        source = next_slab if isinstance(k, int) and k == 0 else lax.rem(slab + z.grid - 2 * k, z.grid)
        return pltpu.make_async_remote_copy(
            src_ref=gathered.at[source], dst_ref=gathered.at[source],
            send_sem=own_send.at[k], recv_sem=own_recv.at[k],
            device_id={"grid": next_slab}, device_id_type=MESH,
        )

    def pass_copy(k):
        source = lax.rem(slab + z.grid - 2 * k, z.grid)
        return pltpu.make_async_remote_copy(
            src_ref=gathered.at[source], dst_ref=gathered.at[source],
            send_sem=pass_send.at[k], recv_sem=pass_recv.at[k],
            device_id={"grid": next_slab}, device_id_type=MESH,
        )

    def pass_arrival(k):
        source = lax.rem(next_slab + z.grid - 2 * k, z.grid)
        return pltpu.make_async_remote_copy(
            src_ref=gathered.at[source], dst_ref=gathered.at[source],
            send_sem=pass_send.at[k], recv_sem=pass_recv.at[k],
            device_id={"grid": next_slab}, device_id_type=MESH,
        )

    near_first = sorted(range(1, far_slabs), key=lambda k: min(k, far_slabs - k))
    for k in near_first:
        own_copy(k).start()
    own_copy(0).start()

    def replicas(piece, rep, rows):
        slot, p = lax.rem(piece // z.pieces, 2), lax.rem(piece, z.pieces)

        def delays_of(r, c):
            return delays[slot, r : r + 16, pl.ds(pl.multiple_of(p * z.piece + c, LANES), LANES)]

        make_replicas(z, tables, delays_of, rep, lax.rem(piece // 2, z.slots), rows)

    def delays_ready(piece):
        @pl.when(lax.rem(piece, z.pieces) == 0)
        def _():
            delay_copy(piece // z.pieces).wait()

    def delays_used(piece):
        after = piece // z.pieces + 2

        @pl.when((lax.rem(piece, z.pieces) == z.pieces - 1) & (after < z.steps))
        def _():
            delay_copy(after).start()

    def early(piece, carry):
        @pl.when(lax.rem(piece, 2) == 0)
        def _():
            delays_ready(piece)
            replicas(piece, rep_even, (0, z.block))

        @pl.when(lax.rem(piece, 2) == 1)
        def _():
            replicas(piece, rep_odd, (0, z.block))
            delays_used(piece)

        return carry

    spots = [z.lead * (n + 1) // (len(near_first) + 2) for n in range(len(near_first))]
    done = 0
    for k, spot in zip(near_first, spots):
        if spot > done:
            lax.fori_loop(done, spot, early, 0)
            done = spot
        own_arrival(k).wait_recv()
        pass_copy(k).start()
    lax.fori_loop(done, z.lead, early, 0)

    own_arrival(0).wait_recv()
    for k in near_first:
        pass_arrival(k).wait_recv()

    spectra_rows = gathered[...].reshape(z.grid * gathered.shape[1], z.chans)
    for g in range(2):
        lo, hi = z.ranges[g]
        lane = lax.broadcasted_iota(jnp.int32, (z.piece, hi - lo), 1) + lo
        sum_sq = jnp.zeros((8, hi - lo), jnp.float32)
        for trig in range(2):
            for p in range(z.pieces):
                part = lax.dot_general(
                    spectra_rows[:, p * z.piece : (p + 1) * z.piece], select[g, trig, :, 0 : hi - lo],
                    (((0,), (0,)), ((), ())), preferred_element_type=jnp.float32,
                )
                if trig == 0:
                    sum_sq += jnp.sum((part * part).reshape(z.piece // 8, 8, hi - lo), axis=0)
                for at in range(z.half):
                    first = (g * z.half + at) * z.per_f
                    row = (2 * at + trig) * z.piece
                    chosen = jnp.where((lane >= first) & (lane < first + z.per_f), part, 0.0)
                    weights[g, p, row : row + z.piece, 0 : hi - lo] = chosen.astype(jnp.bfloat16)
        if g == 0:
            norms[0, :, lo:hi] = sum_sq
            norms[0, :, hi:] = jnp.zeros((8, z.cols - hi), jnp.float32)
        else:
            norms[0, :, lo:hi] += sum_sq

    acc[...] = jnp.zeros_like(acc)

    def norm_copy(k):
        return pltpu.make_async_remote_copy(
            src_ref=norms.at[0], dst_ref=norms.at[k], send_sem=norm_send.at[k], recv_sem=norm_recv.at[k],
            device_id={"chan": lax.rem(me + k, z.chan)}, device_id_type=MESH,
        )

    for k in range(1, z.chan):
        norm_copy(k).start()

    def mate_copy(j, block):
        return pltpu.make_async_remote_copy(
            src_ref=mate_out.at[j, block], dst_ref=mate_in.at[j, block],
            send_sem=mate_send.at[j, block], recv_sem=mate_recv.at[j, block],
            device_id={"chan": mate}, device_id_type=MESH,
        )

    def chip_copy(j, block):
        return pltpu.make_async_remote_copy(
            src_ref=chip_out.at[j, block], dst_ref=chip_in.at[j, block],
            send_sem=chip_send.at[j, block], recv_sem=chip_recv.at[j, block],
            device_id={"chan": chip_at(j) * 2 + core}, device_id_type=MESH,
        )

    def multiply(rep, piece, during):
        slot, p = lax.rem(piece // 2, z.slots), lax.rem(piece, z.pieces)
        for g in range(2):
            lo, hi = z.ranges[g]
            acc[:, lo:hi] += lax.dot_general(
                rep[slot, :, g * half_cols : (g + 1) * half_cols], weights[g, p, :, 0 : hi - lo],
                (((1,), (0,)), ((), ())), preferred_element_type=jnp.float32,
            )
            during(g)

    def turn(piece, rep, ahead_rep):
        ahead = piece + z.lead

        @pl.when(ahead < z.total)
        def _():
            def during(g):
                replicas(ahead, ahead_rep, (g * z.block // 2, (g + 1) * z.block // 2))

            multiply(rep, piece, during)

        @pl.when(ahead >= z.total)
        def _():
            multiply(rep, piece, lambda g: None)

    def pair_step(it, carry):
        step, pair = it // z.pairs, lax.rem(it, z.pairs)

        turn(2 * it, rep_even, rep_odd)
        delays_used(2 * it + z.lead)

        @pl.when(2 * it + 1 + z.lead < z.total)
        def _():
            delays_ready(2 * it + 1 + z.lead)

        turn(2 * it + 1, rep_odd, rep_even)

        @pl.when(pair == z.pairs - 1)
        def _():
            phase, block = step // z.blocks, lax.rem(step, z.blocks)
            j, kind = phase // 2, lax.rem(phase, 2)

            @pl.when(kind == 0)
            def _():
                mate_out[j, block] = acc[...]
                mate_copy(j, block).start()

            @pl.when((kind == 1) & (j < z.chips - 1))
            def _():
                mate_copy(j, block).wait_recv()
                chip_out[j, block] = (acc[...] + mate_in[j, block]).astype(jnp.bfloat16)
                chip_copy(j, block).start()

            @pl.when((kind == 1) & (j == z.chips - 1))
            def _():
                mate_copy(z.chips - 1, block).wait_recv()
                beams = acc[...] + mate_in[z.chips - 1, block]
                for k in range(z.chips - 1):
                    chip_copy(k, block).wait_recv()
                    beams += chip_in[k, block].astype(jnp.float32)
                energy = split_dot(sums[...], beams * beams, 2)
                out[:, pl.ds(pl.multiple_of(block * z.block, z.block), z.block)] = energy

            acc[...] = jnp.zeros_like(acc)

        return carry

    lax.fori_loop(0, z.steps * z.pairs, pair_step, 0)

    for k in range(1, z.chan):
        norm_copy(k).wait()
    total = norms[0]
    for k in range(1, z.chan):
        total += norms[k]
    scale = z.freqs * z.chans * z.chan
    window_norm = jnp.sum(split_dot(sums[...], total, 3), axis=1, keepdims=True) / scale + 1e-06
    out[...] = out[...] / (scale * window_norm)

    own_copy(0).wait_send()
    for k in near_first:
        own_copy(k).wait_send()
        pass_copy(k).wait_send()
    for j in range(z.chips):
        for block in range(z.blocks):
            mate_copy(j, block).wait_send()
            if j < z.chips - 1:
                chip_copy(j, block).wait_send()


def per_device(spectra, travel, quality):
    _, freq_count, own, chans = spectra.shape
    grid_count, chan_count = lax.axis_size("grid"), lax.axis_size("chan")
    z = Sizes(travel.shape[0], chans, freq_count, own * grid_count, grid_count, chan_count)
    mine = jnp.transpose(spectra, (0, 2, 1, 3)).reshape(2 * own * freq_count, chans)
    select = jnp.asarray(selection_matrix(z), jnp.bfloat16)
    tables = jnp.asarray(trig_tables(freq_count))
    sums = jnp.asarray(window_sums(freq_count, z.windows), jnp.bfloat16)
    vmem = pl.BlockSpec(memory_space=pltpu.VMEM)
    far = max(z.chips - 1, 1)
    flops = 2 * z.rows * z.chans * z.cols * 2
    return pl.pallas_call(
        functools.partial(kernel, z),
        out_shape=jax.ShapeDtypeStruct((z.windows, z.rows_out), jnp.float32),
        in_specs=[vmem, vmem, vmem, vmem, vmem, pl.BlockSpec(memory_space=pl.ANY)],
        out_specs=vmem,
        scratch_shapes=[
            pltpu.VMEM((grid_count, 2 * own * freq_count, chans), jnp.bfloat16),
            pltpu.VMEM((2, z.pieces, 2 * z.half * z.piece, z.width), jnp.bfloat16),
            pltpu.VMEM((z.slots, z.block, 2 * z.freqs * z.piece), jnp.bfloat16),
            pltpu.VMEM((z.slots, z.block, 2 * z.freqs * z.piece), jnp.bfloat16),
            pltpu.VMEM((2, z.block, z.chans), jnp.int32),
            pltpu.VMEM((z.block, z.cols), jnp.float32),
            pltpu.VMEM((z.chips, z.blocks, z.block, z.cols), jnp.float32),
            pltpu.VMEM((z.chips, z.blocks, z.block, z.cols), jnp.float32),
            pltpu.VMEM((far, z.blocks, z.block, z.cols), jnp.bfloat16),
            pltpu.VMEM((far, z.blocks, z.block, z.cols), jnp.bfloat16),
            pltpu.VMEM((z.chan, 8, z.cols), jnp.float32),
            pltpu.SemaphoreType.DMA((grid_count // 2,)),
            pltpu.SemaphoreType.DMA((grid_count // 2,)),
            pltpu.SemaphoreType.DMA((grid_count // 2,)),
            pltpu.SemaphoreType.DMA((grid_count // 2,)),
            pltpu.SemaphoreType.DMA((2,)),
            pltpu.SemaphoreType.DMA((z.chips, z.blocks)),
            pltpu.SemaphoreType.DMA((z.chips, z.blocks)),
            pltpu.SemaphoreType.DMA((far, z.blocks)),
            pltpu.SemaphoreType.DMA((far, z.blocks)),
            pltpu.SemaphoreType.DMA((z.chan,)),
            pltpu.SemaphoreType.DMA((z.chan,)),
        ],
        compiler_params=pltpu.CompilerParams(
            collective_id=0, has_side_effects=True, vmem_limit_bytes=56 * 1024 * 1024
        ),
        cost_estimate=pl.CostEstimate(
            flops=flops, bytes_accessed=4 * z.rows * z.chans, transcendentals=0
        ),
        name="beam_power",
    )(mine, quality.reshape(1, chans), select, tables, sums, travel)


def solution(mesh):
    return jax.shard_map(
        per_device,
        mesh=mesh,
        in_specs=(P(None, None, "grid", "chan"), P("grid", "chan"), P("chan")),
        out_specs=P(None, ("grid", "chan")),
        check_vma=False,
    )
```
